1024 devices in a mesh: pipe: 8 (over z_lo), seq: 16 (over y, z_hi), exp: 8 (over x, core).
Axes of the slice: x: 4, y: 8, z: 16 (z_hi: 2, z_lo: 8; z = z_hi * 8 + z_lo), core: 2. Of those that a mesh axis runs over, the one named last changes fastest.
Arguments:
- queries: bfloat16 [8, 8, 2048, 4096], P('pipe', 'exp', 'seq'), may hold values from -160 to 160
- key_rows: bfloat16 [8, 8, 2048, 256], P('pipe', 'exp', 'seq'), may hold values from -160 to 160
- value_rows: bfloat16 [8, 8, 2048, 256], P('pipe', 'exp', 'seq'), may hold values from -6 to 6
- residual: bfloat16 [8, 8, 2048, 4096], P('pipe', 'exp', 'seq'), may hold values from -6 to 6
- doc_lengths: int32 [8, 8, 8], P('pipe', 'exp'), may hold values from 1 to 512, 2048 in all within a row
- norm_gain: float32 [8, 4096], P('pipe'), may hold values from 0.1 to 1.9
- kv_weight: bfloat16 [8, 4096, 512], P('pipe', ('seq', 'exp')), may hold values from -0.09375 to 0.09375
Outputs:
- context: bfloat16 [8, 8, 2048, 4096], P('pipe', 'exp', 'seq')
- kv_next: bfloat16 [8, 8, 2048, 512], P('pipe', 'exp', 'seq')
The draws below stay inside these ranges and needn't reach their ends.
Inputs may be any that keep to these rules, and one draw needn't show every extreme that they name: `doc_lengths`: every pack has a document of exactly 512 tokens and none longer.
All inputs are finite; a program needn't handle non-finite values.
Results may differ from the reference program's by a relative error of at most 0.0058.
Values may be sent and summed in bfloat16 or wider, within the bound.
A program may use at most 64 MiB of HBM per device.

```python
import math
import jax
import jax.numpy as jnp
import numpy as np
from jax import lax

HQ = 32
KVH = 2
DH = 128
NDOC = 8
TOK_DEV = 128
SEGMENTS = 8
PACKS = 8
SHARDS = 16
SEQ_TOK = 2048
MOST = 512


def paired_heads(key):
    key_draw = jax.random.normal(jax.random.fold_in(key, 11), (SEGMENTS, PACKS, SEQ_TOK, KVH, DH), jnp.float32)
    query_draw = jax.random.normal(jax.random.fold_in(key, 12), (SEGMENTS, PACKS, SEQ_TOK, HQ, DH), jnp.float32)
    return (query_draw, key_draw)


def draw_queries(key, part):
    query_draw, key_draw = paired_heads(key)
    return query_draw.reshape(SEGMENTS, PACKS, SEQ_TOK, HQ * DH).astype(jnp.bfloat16)


def draw_key_rows(key, part):
    query_draw, key_draw = paired_heads(key)
    return key_draw.reshape(SEGMENTS, PACKS, SEQ_TOK, KVH * DH).astype(jnp.bfloat16)


def block_levels(stream_key, extent, cuts, low, largest):
    def one(axis_at, shards_of):
        heights = jax.random.uniform(jax.random.fold_in(jax.random.fold_in(stream_key, 6), axis_at), (shards_of,), jnp.float32, low / len(cuts), largest / len(cuts))
        return jnp.repeat(jnp.exp(heights), extent[axis_at] // shards_of).reshape((-1,) + (1,) * (len(extent) - axis_at - 1))

    loudness = one(*cuts[0])
    for cut in cuts[1:]:
        loudness = loudness * one(*cut)
    return loudness


def profile(count, total, most, lean):
    weights = [(1 << 20) // math.isqrt(grade ** lean) + 1 for grade in range(2, count + 1)]
    spare, counts = total - most - (count - 1), [1] * (count - 1)
    while spare > 0:
        movable = [i for i in range(count - 1) if counts[i] < most]
        pool, budget = sum([weights[i] for i in movable]), spare
        for i in movable:
            more = min(most - counts[i], max(1, budget * weights[i] // pool), spare)
            counts[i] = counts[i] + more
            spare = spare - more
    return np.array([most] + counts)


def uneven_parts(own_key, amount, total, bound, skew):
    if amount == 2:
        one = jax.random.randint(own_key, (), max(1, total - bound), min(bound, total - 1) + 1)
        return jnp.stack([one, total - one])
    sizes = jnp.asarray(profile(amount, total, bound, skew), jnp.int32)
    twos = (amount - 1) // 2
    giver, taker = sizes[1:1 + 2 * twos:2], sizes[2:2 + 2 * twos:2]
    room = jnp.minimum(giver - 1, bound - taker)
    passed = jax.random.randint(jax.random.fold_in(own_key, 1), (twos,), 0, 1 << 20) % (room + 1)
    sizes = sizes.at[1:1 + 2 * twos:2].set(giver - passed).at[2:2 + 2 * twos:2].set(taker + passed)
    return sizes[jax.random.permutation(jax.random.fold_in(own_key, 2), amount)]


def scatter_about(rng, extent, scale, bound, split=(), kind=jnp.bfloat16):
    array = scale * jax.random.normal(rng, extent, jnp.float32)
    if split:
        array = array * block_levels(rng, extent, split, -0.22, 0.18)
    return jnp.clip(array, -bound, bound).astype(kind)


def setup_inputs(seed: int = 0) -> dict:
    key_list = jax.random.split(jax.random.key(seed), 8)
    queries = draw_queries(jax.random.fold_in(key_list[7], 71), 0)
    key_rows = draw_key_rows(jax.random.fold_in(key_list[7], 71), 0)
    value_rows = scatter_about(key_list[2], (SEGMENTS, PACKS, SEQ_TOK, KVH * DH), 1.0, 6.0, ((0, 8), (1, 8), (2, 16)))
    residual = scatter_about(key_list[3], (SEGMENTS, PACKS, SEQ_TOK, HQ * DH), 1.0, 6.0, ((0, 8), (1, 8), (2, 16)))
    doc_lengths = jax.vmap(lambda own: uneven_parts(own, NDOC, SEQ_TOK, MOST, 2))(jax.random.split(key_list[4], SEGMENTS * PACKS)).reshape((SEGMENTS, PACKS, NDOC)).astype(jnp.int32)
    norm_gain = jnp.clip(1.0 + 0.18 * jax.random.normal(key_list[5], (SEGMENTS, HQ * DH), jnp.float32), 0.1, 1.9)
    kv_weight = scatter_about(key_list[6], (SEGMENTS, HQ * DH, 2 * KVH * DH), (HQ * DH) ** -0.5, 0.09375, ((0, 8), (1, 128)))
    return {"queries": queries, "key_rows": key_rows, "value_rows": value_rows, "residual": residual, "doc_lengths": doc_lengths, "norm_gain": norm_gain, "kv_weight": kv_weight}


epsilon = 1e-06

def storage_positions(seq_rows, tok_rows, groups):
    index = jnp.arange(seq_rows, dtype=jnp.int32)
    half_rows = tok_rows // 2
    owner_dev = index // tok_rows
    within = index % tok_rows
    return jnp.where(within < half_rows, owner_dev * half_rows + within, (2 * groups - 1 - owner_dev) * half_rows + within - half_rows).astype(jnp.int32)

def reference(queries, key_rows, value_rows, residual, doc_lengths, norm_gain, kv_weight):
    positions = storage_positions(SEQ_TOK, TOK_DEV, SHARDS)
    head_group = HQ // KVH
    score_scale = 1.0 / math.sqrt(DH)
    query_all = queries.reshape(SEGMENTS * PACKS, SEQ_TOK, HQ, DH)
    key_all = key_rows.reshape(SEGMENTS * PACKS, SEQ_TOK, KVH, DH)
    value_all = value_rows.reshape(SEGMENTS * PACKS, SEQ_TOK, KVH, DH)
    length_all = doc_lengths.reshape(SEGMENTS * PACKS, NDOC)

    def one_pack(packed):
        query_pack, key_pack, value_pack, lengths = packed
        bounds = jnp.cumsum(lengths)
        doc_ids = lax.optimization_barrier(jnp.sum((positions[:, None] >= bounds[None, :]).astype(jnp.int32), axis=1))
        visible = (doc_ids[:, None] == doc_ids[None, :]) & (positions[None, :] <= positions[:, None])

        def one_head(head):
            query_head = lax.dynamic_index_in_dim(query_pack, head, 1, keepdims=False)
            key_head = lax.dynamic_index_in_dim(key_pack, head // head_group, 1, keepdims=False)
            value_head = lax.dynamic_index_in_dim(value_pack, head // head_group, 1, keepdims=False)
            scores = jnp.dot(query_head, key_head.T, preferred_element_type=jnp.float32) * score_scale
            scores = jnp.where(visible, scores, -1e+30)
            row_max = lax.optimization_barrier(jnp.max(scores, axis=1, keepdims=True))
            weights = jnp.where(visible, jnp.exp(scores - row_max), 0.0)
            sums = lax.optimization_barrier(jnp.sum(weights, axis=1, keepdims=True))
            mixed_rows = jnp.dot(weights.astype(jnp.bfloat16), value_head, preferred_element_type=jnp.float32)
            return (mixed_rows / sums).astype(jnp.bfloat16)
        heads_out = lax.map(one_head, jnp.arange(HQ, dtype=jnp.int32))
        return jnp.transpose(heads_out, (1, 0, 2)).reshape(SEQ_TOK, HQ * DH)
    context = lax.map(one_pack, (query_all, key_all, value_all, length_all))
    context = context.reshape(SEGMENTS, PACKS, SEQ_TOK, HQ * DH)
    layer_out = (residual.astype(jnp.float32) + context.astype(jnp.float32)).astype(jnp.bfloat16)
    received = jnp.concatenate([jnp.zeros_like(layer_out[:1]), layer_out[:-1]], axis=0)
    as_float = received.astype(jnp.float32)
    mean_square = lax.optimization_barrier(jnp.mean(as_float * as_float, axis=3, keepdims=True))
    normed = (as_float * lax.rsqrt(mean_square + epsilon) * norm_gain[:, None, None, :]).astype(jnp.bfloat16)

    def project(packed):
        normed_segment, weight_segment = packed
        return jnp.dot(normed_segment, weight_segment, preferred_element_type=jnp.float32).astype(jnp.bfloat16)
    kv_next = lax.map(project, (normed.reshape(SEGMENTS, PACKS * SEQ_TOK, HQ * DH), kv_weight))
    return (context, kv_next.reshape(SEGMENTS, PACKS, SEQ_TOK, 2 * KVH * DH))
```

```python
import functools
import math

import jax
import jax.numpy as jnp
from jax import lax
from jax.experimental import pallas as pl
from jax.experimental.pallas import tpu as pltpu
from jax.sharding import Mesh
from jax.sharding import PartitionSpec as P

MESH = pl.DeviceIdType.MESH
NAMES = ("pipe", "y", "zh", "x", "c")
SECTIONS, YS, ZHS, XS, CORES = 8, 8, 2, 4, 2
EXPS = XS * CORES
ROWS, HALF, DH = 128, 64, 128
WIDTH, HEADS, KVH = 4096, 32, 2
KV = 2 * KVH * DH
PART = KV // CORES
NDOC = 8
REACH = 5
KEYS = REACH * ROWS
SHARD = 32
EPSILON = 1e-06
HIDDEN = -1e30
CHUNK = 4
LOG2E = 1.4426950408889634


def kernel(
    q_hbm, k_hbm, v_hbm, r_hbm, dl_ref, g_hbm, w_hbm, ctx_hbm, kv_hbm,
    fbuf, tbuf, wbuf, gbuf, qv, rv, cv, lo, bias, ov,
    send_sems, load_sems, out_sems, z_recv, f_recv, t_recv, wz_recv, wy_recv,
    wx_recv, lo_recv, g_recv, o_recv,
):
    pipe, y, zh = lax.axis_index("pipe"), lax.axis_index("y"), lax.axis_index("zh")
    x, c = lax.axis_index("x"), lax.axis_index("c")
    z = zh * SECTIONS + pipe

    def at_z(step):
        there = lax.rem(z + step, SECTIONS * ZHS)
        return {"pipe": lax.rem(there, SECTIONS), "zh": there // SECTIONS}

    def at_y(step):
        return {"y": lax.rem(y + step + YS, YS)}

    def at_x(step):
        return {"x": lax.rem(x + step, XS)}

    twin = {"c": 1 - c}
    partner = {"zh": 1 - zh}
    behind, far_behind = at_z(15), at_z(7)
    ahead, far_ahead = at_z(1), at_z(9)

    pending = []

    def when(cond, act):
        if cond is None:
            act()
        else:
            pl.when(cond)(act)

    def send(src, dst, recv, dev, cond=None):
        index = len(pending)

        def make():
            return pltpu.make_async_remote_copy(
                src_ref=src, dst_ref=dst, send_sem=send_sems.at[index],
                recv_sem=recv, device_id=dev, device_id_type=MESH,
            )

        when(cond, lambda: make().start())
        pending.append((cond, make))

    def arrive(dst, recv, cond=None):
        def act():
            pltpu.make_async_remote_copy(
                src_ref=dst, dst_ref=dst, send_sem=send_sems.at[0],
                recv_sem=recv, device_id=twin, device_id_type=MESH,
            ).wait_recv()

        when(cond, act)

    loads = [
        (k_hbm.at[:HALF], fbuf.at[0, zh, :, : KVH * DH]),
        (v_hbm.at[:HALF], fbuf.at[0, zh, :, KVH * DH :]),
        (k_hbm.at[HALF:], tbuf.at[0, 1 - zh, :, : KVH * DH]),
        (v_hbm.at[HALF:], tbuf.at[0, 1 - zh, :, KVH * DH :]),
        (q_hbm, qv),
        (r_hbm, rv),
    ]
    loads = [pltpu.make_async_copy(a, b, load_sems.at[i]) for i, (a, b) in enumerate(loads)]
    for load in loads:
        load.start()

    barrier = pltpu.get_barrier_semaphore()
    greeted = [partner, twin] + [at_y(k) for k in (1, -1, 3, -3)] + [at_x(k) for k in (1, 2, 3)]
    for place in (behind, far_behind, ahead, far_ahead):
        greeted += [{**place, "c": core} for core in range(CORES)]
    for dev in greeted:
        pl.semaphore_signal(barrier, inc=1, device_id=dev, device_id_type=MESH)
    spill = [(7, 6, 2), (7, 5, 3), (7, 4, 4), (6, 5, 4)]
    for a, b in ((7, 5), (5, 7)):
        @pl.when(y == a)
        def _():
            pl.semaphore_signal(barrier, inc=1, device_id={"y": b}, device_id_type=MESH)

    for d in range(1, REACH):
        @pl.when(y < d)
        def _():
            fbuf[d] = jnp.zeros(fbuf.shape[1:], fbuf.dtype)

    row = lax.broadcasted_iota(jnp.int32, (HALF, 1), 0)
    lane = lax.broadcasted_iota(jnp.int32, (1, KEYS), 1)
    shard = y * ZHS + zh
    for run in range(2):
        query_pos = row + (shard if run == 0 else 2 * YS * ZHS - 1 - shard) * HALF
        top = y if run == 0 else 2 * YS - 1 - y
        key_pos = top * ROWS + lax.rem(lane, ROWS) - ROWS * lax.div(lane, ROWS)
        bound, first = jnp.int32(0), jnp.zeros((HALF, 1), jnp.int32)
        for doc in range(NDOC):
            bound = bound + dl_ref[doc]
            first = jnp.where(query_pos >= bound, bound, first)
        seen = (key_pos >= first) & (key_pos <= query_pos)
        bias[run] = jnp.where(seen, 0.0, HIDDEN)

    extra = jnp.where((y == 7) | (y == 5), 1, 0)
    pl.semaphore_wait(barrier, len(greeted) + extra)

    e = x * CORES + c
    for core in range(CORES):
        for place in (behind, far_behind):
            send(w_hbm.at[:, pl.ds(core * PART, PART)], wbuf.at[y, zh, e], wz_recv.at[zh, c], {**place, "c": core})
    for load in loads[:4]:
        load.wait()
    send(fbuf.at[0, zh], fbuf.at[0, zh], z_recv.at[0], partner)
    send(tbuf.at[0, 1 - zh], tbuf.at[0, 1 - zh], z_recv.at[1], partner)

    def copies(at, shift, d, half):
        slot = d + shift
        if slot < REACH:
            @pl.when(y == at)
            def _():
                pltpu.make_async_copy(fbuf.at[d, half], tbuf.at[slot, half], t_recv.at[slot, half]).start()

    def first_from_own(half):
        for k in (1, 3):
            send(fbuf.at[0, half], fbuf.at[k, half], f_recv.at[k, half], at_y(k), y + k < YS)
        for src, dst, slot in spill:
            send(fbuf.at[0, half], tbuf.at[slot, half], t_recv.at[slot, half], {"y": dst}, y == src)
        copies(7, 1, 0, half)
        copies(6, 3, 0, half)

    def second_from_own(half):
        for k in (1, 3):
            send(tbuf.at[0, half], tbuf.at[k, half], t_recv.at[k, half], at_y(-k), y >= k)

    def first_on(d, half):
        arrive(fbuf.at[d, half], f_recv.at[d, half], y >= d)
        if d % 2 == 1:
            send(fbuf.at[d, half], fbuf.at[d + 1, half], f_recv.at[d + 1, half], at_y(1), (y >= d) & (y + 1 < YS))
        copies(7, 1, d, half)
        copies(6, 3, d, half)

    def second_on(d, half):
        arrive(tbuf.at[d, half], t_recv.at[d, half], y + d < YS)
        if d % 2 == 1:
            send(tbuf.at[d, half], tbuf.at[d + 1, half], t_recv.at[d + 1, half], at_y(-1), (y + d < YS) & (y > 0))

    def w_part(r, side):
        return wbuf.at[lax.rem(y + YS - r, YS), :, pl.ds(lax.rem(x + side, XS) * CORES, CORES)]

    def w_along_x(r):
        part = w_part(r, 0)
        for k in range(1, XS):
            send(part, part, wx_recv.at[r, XS - k], at_x(k))

    def w_start():
        for h in range(ZHS):
            for core in range(CORES):
                arrive(wbuf.at[y, h, x * CORES + core], wz_recv.at[h, core])
        part = w_part(0, 0)
        for k in (1, -1, 3, -3):
            send(part, part, wy_recv.at[k % YS], at_y(k))
        w_along_x(0)

    def w_on(r):
        part = w_part(r, 0)
        arrive(part, wy_recv.at[r])
        if r in (1, 3):
            send(part, part, wy_recv.at[r + 1], at_y(1))
        if r == 7:
            send(part, part, wy_recv.at[r - 1], at_y(-1))
        w_along_x(r)

    own, other = zh, 1 - zh
    first_from_own(own)
    second_from_own(other)
    send(g_hbm, gbuf, g_recv, behind)
    for d in (1, 3):
        first_on(d, own)
        second_on(d, other)
    w_start()
    arrive(fbuf.at[0, other], z_recv.at[0])
    first_from_own(other)
    arrive(tbuf.at[0, own], z_recv.at[1])
    second_from_own(own)
    for r in (1, 7, 3, 5):
        w_on(r)
    for d in (1, 3):
        first_on(d, other)
        second_on(d, own)
    for r in (2, 6, 4):
        w_on(r)
    for d in (2, 4):
        for half in range(2):
            first_on(d, half)
    for load in loads[4:]:
        load.wait()

    scale = LOG2E / math.sqrt(DH)
    last = pipe == SECTIONS - 1
    ones = jnp.ones((KEYS, DH), jnp.bfloat16)

    def attend(run, group):
        buf = fbuf if run == 0 else tbuf
        own_lo = lo.at[c]
        rows = pl.ds(run * HALF, HALF)
        keys = buf[:, :, :, pl.ds(group * DH, DH)].reshape(KEYS, DH)
        values = buf[:, :, :, pl.ds((KVH + group) * DH, DH)].reshape(KEYS, DH)
        values = jnp.concatenate([values, ones], axis=1)
        per_group = HEADS // KVH

        def step(j, carry):
            base = (group * per_group + j * CHUNK) * DH
            cols = [pl.ds(pl.multiple_of(base + i * DH, DH), DH) for i in range(CHUNK)]
            queries = jnp.concatenate([qv[rows, col] for col in cols], axis=0)
            scores = lax.dot_general(
                queries, keys, (((1,), (1,)), ((), ())), preferred_element_type=jnp.float32
            )
            scores = scores.reshape(CHUNK, HALF, KEYS) * scale + bias[run]
            weights = jnp.exp2(scores - jnp.max(scores, axis=2, keepdims=True))
            rounded = weights.astype(jnp.bfloat16).reshape(CHUNK * HALF, KEYS)
            mixed = jnp.dot(rounded, values, preferred_element_type=jnp.float32)
            mixed = (mixed[:, :DH] / mixed[:, DH:]).astype(jnp.bfloat16)
            for i, col in enumerate(cols):
                context = mixed[i * HALF : (i + 1) * HALF]
                cv[rows, col] = context
                out = (rv[rows, col].astype(jnp.float32) + context.astype(jnp.float32)).astype(jnp.bfloat16)
                out = jnp.where(last, jnp.zeros_like(out), out)
                own_lo[rows, col] = out
            return carry

        lax.fori_loop(0, per_group // CHUNK, step, 0)
        part = lo.at[c, rows, pl.ds(group * per_group * DH, per_group * DH)]
        send(part, part, lo_recv.at[run, group], twin)

    outs = [
        pltpu.make_async_copy(cv.at[pl.ds(run * HALF, HALF)], ctx_hbm.at[pl.ds(run * HALF, HALF)], out_sems.at[run])
        for run in range(2)
    ]
    attend(0, 0)
    attend(0, 1)
    outs[0].start()
    for d in (2, 4):
        for half in range(2):
            second_on(d, half)
    for d in range(1, REACH):
        for half in range(2):
            arrive(tbuf.at[d, half], t_recv.at[d, half], y + d >= YS)
    attend(1, 0)
    attend(1, 1)
    outs[1].start()
    arrive(gbuf, g_recv)
    for r in range(YS):
        for side in range(1, XS):
            arrive(w_part(r, side), wx_recv.at[r, side])
    for run in range(2):
        for group in range(KVH):
            part = lo.at[1 - c, pl.ds(run * HALF, HALF), pl.ds(group * (WIDTH // KVH), WIDTH // KVH)]
            arrive(part, lo_recv.at[run, group])

    tokens = CORES * ROWS
    squares = jnp.zeros((tokens, DH), jnp.float32)
    for i in range(WIDTH // DH):
        part = lo[:, :, pl.ds(i * DH, DH)].reshape(tokens, DH).astype(jnp.float32)
        squares = squares + part * part
    inverse = lax.rsqrt(jnp.sum(squares, axis=1, keepdims=True) / WIDTH + EPSILON)
    total = jnp.zeros((tokens, PART), jnp.float32)
    depth = WIDTH // YS
    for i in range(YS):
        cols = pl.ds(i * depth, depth)
        part = lo[:, :, cols].reshape(tokens, depth).astype(jnp.float32)
        normed = (part * inverse * gbuf[:, cols]).astype(jnp.bfloat16)
        total = total + jnp.dot(normed, wbuf[i].reshape(depth, PART), preferred_element_type=jnp.float32)
    ov[...] = total.astype(jnp.bfloat16).reshape(CORES, ROWS, PART)
    mine = kv_hbm.at[:, pl.ds(pl.multiple_of(c * PART, PART), PART)]
    for core in range(CORES):
        send(ov.at[core], mine, o_recv.at[c], {**ahead, "c": core})
    for out in outs:
        out.wait()
    for core in range(CORES):
        arrive(kv_hbm.at[:, pl.ds(core * PART, PART)], o_recv.at[core])
    for cond, make in pending:
        when(cond, lambda: make().wait_send())


def on_device(queries, key_rows, value_rows, residual, doc_lengths, norm_gain, kv_weight):
    bf16, f32 = jnp.bfloat16, jnp.float32
    anywhere = pl.BlockSpec(memory_space=pl.ANY)
    dma = pltpu.SemaphoreType.DMA
    context, kv_next = pl.pallas_call(
        kernel,
        out_shape=(
            jax.ShapeDtypeStruct((ROWS, WIDTH), bf16),
            jax.ShapeDtypeStruct((ROWS, KV), bf16),
        ),
        in_specs=[anywhere] * 4 + [pl.BlockSpec(memory_space=pltpu.SMEM)] + [anywhere] * 2,
        out_specs=(anywhere, anywhere),
        scratch_shapes=[
            pltpu.VMEM((REACH, ZHS, HALF, KV), bf16),
            pltpu.VMEM((REACH, ZHS, HALF, KV), bf16),
            pltpu.VMEM((YS, ZHS, EXPS, SHARD, PART), bf16),
            pltpu.VMEM((1, WIDTH), f32),
            pltpu.VMEM((ROWS, WIDTH), bf16),
            pltpu.VMEM((ROWS, WIDTH), bf16),
            pltpu.VMEM((ROWS, WIDTH), bf16),
            pltpu.VMEM((CORES, ROWS, WIDTH), bf16),
            pltpu.VMEM((2, HALF, KEYS), f32),
            pltpu.VMEM((CORES, ROWS, PART), bf16),
            dma((96,)),
            dma((6,)),
            dma((2,)),
            dma((2,)),
            dma((REACH, ZHS)),
            dma((REACH, ZHS)),
            dma((ZHS, CORES)),
            dma((YS,)),
            dma((YS, XS)),
            dma((2, KVH)),
            dma(()),
            dma((CORES,)),
        ],
        compiler_params=pltpu.CompilerParams(
            collective_id=0, has_side_effects=True, vmem_limit_bytes=60 * 2**20
        ),
    )(
        queries.reshape(ROWS, WIDTH),
        key_rows.reshape(ROWS, KVH * DH),
        value_rows.reshape(ROWS, KVH * DH),
        residual.reshape(ROWS, WIDTH),
        doc_lengths.reshape(NDOC),
        norm_gain,
        kv_weight.reshape(SHARD, KV),
    )
    return context.reshape(1, 1, ROWS, WIDTH), kv_next.reshape(1, 1, ROWS, KV)


def solution(mesh):
    finer = Mesh(mesh.devices.reshape(SECTIONS, YS, ZHS, XS, CORES), NAMES)
    tokens = P("pipe", ("x", "c"), ("y", "zh"), None)
    return jax.shard_map(
        on_device,
        mesh=finer,
        in_specs=(
            tokens, tokens, tokens, tokens,
            P("pipe", ("x", "c"), None),
            P("pipe", None),
            P("pipe", ("y", "zh", "x", "c"), None),
        ),
        out_specs=(tokens, tokens),
        check_vma=False,
    )
```

```python
import functools
import math

import jax
import jax.numpy as jnp
from jax import lax
from jax.experimental import pallas as pl
from jax.experimental.pallas import tpu as pltpu
from jax.sharding import Mesh
from jax.sharding import PartitionSpec as P

MESH = pl.DeviceIdType.MESH
NAMES = ("pipe", "y", "zh", "x", "c")
SECTIONS, YS, ZHS, XS, CORES = 8, 8, 2, 4, 2
EXPS = XS * CORES
ROWS, HALF, DH = 128, 64, 128
WIDTH, HEADS, KVH = 4096, 32, 2
KV = 2 * KVH * DH
PART = KV // CORES
NDOC = 8
REACH = 5
KEYS = REACH * ROWS
SHARD = 32
EPSILON = 1e-06
HIDDEN = -1e30
CHUNK = 16
LOG2E = 1.4426950408889634


def kernel(
    q_hbm, k_hbm, v_hbm, r_hbm, dl_hbm, g_hbm, w_hbm, ctx_hbm, kv_hbm,
    fbuf, tbuf, wbuf, gbuf, qv, rv, cv, lo, bias, ov, keys_t, values_one, ss, dl_ref, wv,
    send_sems, load_sems, out_sems, z_recv, f_recv, t_recv, wz_recv, wy_recv,
    wx_recv, lo_recv, g_recv, o_recv,
):
    pipe, y, zh = lax.axis_index("pipe"), lax.axis_index("y"), lax.axis_index("zh")
    x, c = lax.axis_index("x"), lax.axis_index("c")
    z = zh * SECTIONS + pipe

    def at_z(step):
        there = lax.rem(z + step, SECTIONS * ZHS)
        return {"pipe": lax.rem(there, SECTIONS), "zh": there // SECTIONS}

    def at_y(step):
        return {"y": lax.rem(y + step + YS, YS)}

    def at_x(step):
        return {"x": lax.rem(x + step, XS)}

    twin = {"c": 1 - c}
    partner = {"zh": 1 - zh}
    behind, far_behind = at_z(15), at_z(7)
    ahead, far_ahead = at_z(1), at_z(9)

    pending = []

    def when(cond, act):
        if cond is None:
            act()
        else:
            pl.when(cond)(act)

    def send(src, dst, recv, dev, cond=None):
        index = len(pending)

        def make():
            return pltpu.make_async_remote_copy(
                src_ref=src, dst_ref=dst, send_sem=send_sems.at[index],
                recv_sem=recv, device_id=dev, device_id_type=MESH,
            )

        when(cond, lambda: make().start())
        pending.append((cond, make))

    def arrive(dst, recv, cond=None):
        def act():
            pltpu.make_async_remote_copy(
                src_ref=dst, dst_ref=dst, send_sem=send_sems.at[0],
                recv_sem=recv, device_id=twin, device_id_type=MESH,
            ).wait_recv()

        when(cond, act)

    barrier = pltpu.get_barrier_semaphore()
    greeted = [partner, twin] + [at_y(k) for k in (1, -1, 3, -3)] + [at_x(k) for k in (1, 2, 3)]
    for place in (behind, far_behind, ahead, far_ahead):
        greeted += [{**place, "c": core} for core in range(CORES)]
    for dev in greeted:
        pl.semaphore_signal(barrier, inc=1, device_id=dev, device_id_type=MESH)
    spill = [(7, 6, 2), (7, 5, 3), (7, 4, 4), (6, 5, 4)]
    for a, b in ((7, 5), (5, 7)):
        @pl.when(y == a)
        def _():
            pl.semaphore_signal(barrier, inc=1, device_id={"y": b}, device_id_type=MESH)

    loads = [
        (k_hbm.at[:HALF], fbuf.at[0, zh, :, : KVH * DH]),
        (v_hbm.at[:HALF], fbuf.at[0, zh, :, KVH * DH :]),
        (k_hbm.at[HALF:], tbuf.at[0, 1 - zh, :, : KVH * DH]),
        (v_hbm.at[HALF:], tbuf.at[0, 1 - zh, :, KVH * DH :]),
        (dl_hbm, dl_ref),
        (w_hbm.at[:, :PART], wv.at[0]),
        (w_hbm.at[:, PART:], wv.at[1]),
        (q_hbm, qv),
        (r_hbm, rv),
    ]
    loads = [pltpu.make_async_copy(a, b, load_sems.at[i]) for i, (a, b) in enumerate(loads)]
    for load in loads:
        load.start()

    for d in range(1, REACH):
        @pl.when(y < d)
        def _():
            fbuf[d] = jnp.zeros(fbuf.shape[1:], fbuf.dtype)

    loads[4].wait()
    row = lax.broadcasted_iota(jnp.int32, (HALF, 1), 0)
    lane = lax.broadcasted_iota(jnp.int32, (1, KEYS), 1)
    shard = y * ZHS + zh
    for run in range(2):
        query_pos = row + (shard if run == 0 else 2 * YS * ZHS - 1 - shard) * HALF
        top = y if run == 0 else 2 * YS - 1 - y
        key_pos = top * ROWS + lax.rem(lane, ROWS) - ROWS * lax.div(lane, ROWS)
        bound, first = jnp.int32(0), jnp.zeros((HALF, 1), jnp.int32)
        for doc in range(NDOC):
            bound = bound + dl_ref[0, doc]
            first = jnp.where(query_pos >= bound, bound, first)
        seen = (key_pos >= first) & (key_pos <= query_pos)
        bias[run] = jnp.where(seen, 0.0, HIDDEN)

    extra = jnp.where((y == 7) | (y == 5), 1, 0)
    pl.semaphore_wait(barrier, len(greeted) + extra)

    for load in loads[5:7]:
        load.wait()
    for core in range(CORES):
        for place in (behind, far_behind):
            send(wv.at[core], wbuf.at[y, x, zh, c], wz_recv.at[zh, c], {**place, "c": core})
    for load in loads[:4]:
        load.wait()
    send(fbuf.at[0, zh], fbuf.at[0, zh], z_recv.at[0], partner)
    send(tbuf.at[0, 1 - zh], tbuf.at[0, 1 - zh], z_recv.at[1], partner)

    def copies(at, shift, d, half):
        slot = d + shift
        if slot < REACH:
            @pl.when(y == at)
            def _():
                pltpu.make_async_copy(fbuf.at[d, half], tbuf.at[slot, half], t_recv.at[slot, half]).start()

    def first_from_own(half):
        for k in (1, 3):
            send(fbuf.at[0, half], fbuf.at[k, half], f_recv.at[k, half], at_y(k), y + k < YS)
        for src, dst, slot in spill:
            send(fbuf.at[0, half], tbuf.at[slot, half], t_recv.at[slot, half], {"y": dst}, y == src)
        copies(7, 1, 0, half)
        copies(6, 3, 0, half)

    def second_from_own(half):
        for k in (1, 3):
            send(tbuf.at[0, half], tbuf.at[k, half], t_recv.at[k, half], at_y(-k), y >= k)

    def first_on(d, half):
        arrive(fbuf.at[d, half], f_recv.at[d, half], y >= d)
        if d % 2 == 1:
            send(fbuf.at[d, half], fbuf.at[d + 1, half], f_recv.at[d + 1, half], at_y(1), (y >= d) & (y + 1 < YS))
        copies(7, 1, d, half)
        copies(6, 3, d, half)

    def second_on(d, half):
        arrive(tbuf.at[d, half], t_recv.at[d, half], y + d < YS)
        if d % 2 == 1:
            send(tbuf.at[d, half], tbuf.at[d + 1, half], t_recv.at[d + 1, half], at_y(-1), (y + d < YS) & (y > 0))

    def w_part(r, side):
        return wbuf.at[lax.rem(y + YS - r, YS), lax.rem(x + side, XS)]

    def w_along_x(r):
        part = w_part(r, 0)
        for k in range(1, XS):
            send(part, part, wx_recv.at[r, XS - k], at_x(k))

    def w_start(h):
        for core in range(CORES):
            arrive(wbuf.at[y, x, h, core], wz_recv.at[h, core])
        part = w_part(0, 0).at[h]
        for k in (1, -1, 3, -3):
            send(part, part, wy_recv.at[k % YS, h], at_y(k))

    def w_on(r, h):
        part = w_part(r, 0).at[h]
        arrive(part, wy_recv.at[r, h])
        if r in (1, 3):
            send(part, part, wy_recv.at[r + 1, h], at_y(1))
        if r == 7:
            send(part, part, wy_recv.at[r - 1, h], at_y(-1))

    own, other = zh, 1 - zh
    first_from_own(own)
    second_from_own(other)
    send(g_hbm, gbuf, g_recv, behind)
    ss[...] = jnp.zeros_like(ss)
    near, far = ahead["zh"], 1 - ahead["zh"]
    w_start(near)
    for d in (1, 3):
        first_on(d, own)
        second_on(d, other)
    w_start(far)
    w_along_x(0)
    for r in (1, 7, 3, 5):
        w_on(r, near)
    arrive(fbuf.at[0, other], z_recv.at[0])
    first_from_own(other)
    for r in (1, 7, 3, 5):
        w_on(r, far)
        w_along_x(r)
    arrive(tbuf.at[0, own], z_recv.at[1])
    second_from_own(own)
    for d in (1, 3):
        first_on(d, other)
        second_on(d, own)
    for r in (2, 6, 4):
        w_on(r, near)
        w_on(r, far)
        w_along_x(r)
    for d in (2, 4):
        for half in range(2):
            first_on(d, half)
    for load in loads[7:]:
        load.wait()

    scale = LOG2E / math.sqrt(DH)
    last = pipe == SECTIONS - 1
    ones = jnp.ones((KEYS, DH), jnp.bfloat16)

    def add_squares(core, run, group):
        rows = pl.ds(run * HALF, HALF)
        found = ss[core, rows]
        for i in range(HEADS // KVH):
            out = lo[core, rows, pl.ds((group * (HEADS // KVH) + i) * DH, DH)].astype(jnp.float32)
            found = found + out * out
        ss[core, rows] = found

    def from_twin(run, group):
        part = lo.at[1 - c, pl.ds(run * HALF, HALF), pl.ds(group * (WIDTH // KVH), WIDTH // KVH)]
        arrive(part, lo_recv.at[run, group])
        add_squares(1 - c, run, group)

    def attend(run, group):
        buf = fbuf if run == 0 else tbuf
        own_lo = lo.at[c]
        rows = pl.ds(run * HALF, HALF)
        keys = buf[:, :, :, pl.ds(group * DH, DH)].reshape(KEYS, DH)
        values = buf[:, :, :, pl.ds((KVH + group) * DH, DH)].reshape(KEYS, DH)
        keys_t[...] = keys.T
        values_one[:, :DH] = values
        values_one[:, DH:] = ones
        per_group = HEADS // KVH

        def step(j, carry):
            base = (group * per_group + j * CHUNK) * DH
            cols = [pl.ds(pl.multiple_of(base + i * DH, DH), DH) for i in range(CHUNK)]
            queries = jnp.concatenate([qv[rows, col] for col in cols], axis=0)
            scores = jnp.dot(queries, keys_t[...], preferred_element_type=jnp.float32)
            scores = scores.reshape(CHUNK, HALF, KEYS) * scale + bias[run]
            weights = jnp.exp2(scores - jnp.max(scores, axis=2, keepdims=True))
            rounded = weights.astype(jnp.bfloat16).reshape(CHUNK * HALF, KEYS)
            mixed = jnp.dot(rounded, values_one[...], preferred_element_type=jnp.float32)
            mixed = (mixed[:, :DH] / mixed[:, DH:]).astype(jnp.bfloat16)
            for i, col in enumerate(cols):
                context = mixed[i * HALF : (i + 1) * HALF]
                cv[rows, col] = context
                out = (rv[rows, col].astype(jnp.float32) + context.astype(jnp.float32)).astype(jnp.bfloat16)
                out = jnp.where(last, jnp.zeros_like(out), out)
                own_lo[rows, col] = out
            return carry

        lax.fori_loop(0, per_group // CHUNK, step, 0)
        part = lo.at[c, rows, pl.ds(group * per_group * DH, per_group * DH)]
        send(part, part, lo_recv.at[run, group], twin)
        add_squares(c, run, group)

    outs = [
        pltpu.make_async_copy(cv.at[pl.ds(run * HALF, HALF)], ctx_hbm.at[pl.ds(run * HALF, HALF)], out_sems.at[run])
        for run in range(2)
    ]
    attend(0, 0)
    attend(0, 1)
    outs[0].start()
    for d in (2, 4):
        for half in range(2):
            second_on(d, half)
    for d in range(1, REACH):
        for half in range(2):
            arrive(tbuf.at[d, half], t_recv.at[d, half], y + d >= YS)
    attend(1, 0)
    from_twin(0, 0)
    from_twin(0, 1)
    attend(1, 1)
    outs[1].start()
    from_twin(1, 0)
    arrive(gbuf, g_recv)
    for r in range(YS):
        for side in range(1, XS):
            arrive(w_part(r, side), wx_recv.at[r, side])
    from_twin(1, 1)

    tokens = CORES * ROWS
    squares = jnp.sum(ss[...].reshape(tokens, DH), axis=1, keepdims=True)
    inverse = lax.rsqrt(squares / WIDTH + EPSILON)
    total = jnp.zeros((tokens, PART), jnp.float32)
    depth = WIDTH // YS
    for i in range(YS):
        cols = pl.ds(i * depth, depth)
        part = lo[:, :, cols].reshape(tokens, depth).astype(jnp.float32)
        weights = [wbuf[i, j, h].reshape(CORES * SHARD, PART) for h in range(ZHS) for j in range(XS)]
        weights = jnp.concatenate(weights, axis=0)
        normed = (part * inverse * gbuf[:, cols]).astype(jnp.bfloat16)
        total = total + jnp.dot(normed, weights, preferred_element_type=jnp.float32)
    ov[...] = total.astype(jnp.bfloat16).reshape(CORES, ROWS, PART)
    mine = kv_hbm.at[:, pl.ds(pl.multiple_of(c * PART, PART), PART)]
    for core in range(CORES):
        send(ov.at[core], mine, o_recv.at[c], {**ahead, "c": core})
    for out in outs:
        out.wait()
    for core in range(CORES):
        arrive(kv_hbm.at[:, pl.ds(core * PART, PART)], o_recv.at[core])
    for cond, make in pending:
        when(cond, lambda: make().wait_send())


def on_device(queries, key_rows, value_rows, residual, doc_lengths, norm_gain, kv_weight):
    bf16, f32 = jnp.bfloat16, jnp.float32
    anywhere = pl.BlockSpec(memory_space=pl.ANY)
    dma = pltpu.SemaphoreType.DMA
    context, kv_next = pl.pallas_call(
        kernel,
        out_shape=(
            jax.ShapeDtypeStruct((ROWS, WIDTH), bf16),
            jax.ShapeDtypeStruct((ROWS, KV), bf16),
        ),
        in_specs=[anywhere] * 4 + [anywhere] + [anywhere] * 2,
        out_specs=(anywhere, anywhere),
        scratch_shapes=[
            pltpu.VMEM((REACH, ZHS, HALF, KV), bf16),
            pltpu.VMEM((REACH, ZHS, HALF, KV), bf16),
            pltpu.VMEM((YS, XS, ZHS, CORES, SHARD, PART), bf16),
            pltpu.VMEM((1, WIDTH), f32),
            pltpu.VMEM((ROWS, WIDTH), bf16),
            pltpu.VMEM((ROWS, WIDTH), bf16),
            pltpu.VMEM((ROWS, WIDTH), bf16),
            pltpu.VMEM((CORES, ROWS, WIDTH), bf16),
            pltpu.VMEM((2, HALF, KEYS), f32),
            pltpu.VMEM((CORES, ROWS, PART), bf16),
            pltpu.VMEM((DH, KEYS), bf16),
            pltpu.VMEM((KEYS, 2 * DH), bf16),
            pltpu.VMEM((CORES, ROWS, DH), f32),
            pltpu.SMEM((1, NDOC), jnp.int32),
            pltpu.VMEM((CORES, SHARD, PART), bf16),
            dma((96,)),
            dma((9,)),
            dma((2,)),
            dma((2,)),
            dma((REACH, ZHS)),
            dma((REACH, ZHS)),
            dma((ZHS, CORES)),
            dma((YS, ZHS)),
            dma((YS, XS)),
            dma((2, KVH)),
            dma(()),
            dma((CORES,)),
        ],
        compiler_params=pltpu.CompilerParams(
            collective_id=0, has_side_effects=True, vmem_limit_bytes=60 * 2**20
        ),
    )(
        queries.reshape(ROWS, WIDTH),
        key_rows.reshape(ROWS, KVH * DH),
        value_rows.reshape(ROWS, KVH * DH),
        residual.reshape(ROWS, WIDTH),
        doc_lengths.reshape(1, NDOC),
        norm_gain,
        kv_weight.reshape(SHARD, KV),
    )
    return context.reshape(1, 1, ROWS, WIDTH), kv_next.reshape(1, 1, ROWS, KV)


def solution(mesh):
    finer = Mesh(mesh.devices.reshape(SECTIONS, YS, ZHS, XS, CORES), NAMES)
    tokens = P("pipe", ("x", "c"), ("y", "zh"), None)
    return jax.shard_map(
        on_device,
        mesh=finer,
        in_specs=(
            tokens, tokens, tokens, tokens,
            P("pipe", ("x", "c"), None),
            P("pipe", None),
            P("pipe", ("y", "zh", "x", "c"), None),
        ),
        out_specs=(tokens, tokens),
        check_vma=False,
    )
```

```python
import functools
import math

import jax
import jax.numpy as jnp
from jax import lax
from jax.experimental import pallas as pl
from jax.experimental.pallas import tpu as pltpu
from jax.sharding import Mesh
from jax.sharding import PartitionSpec as P

MESH = pl.DeviceIdType.MESH
NAMES = ("pipe", "y", "zh", "x", "c")
SECTIONS, YS, ZHS, XS, CORES = 8, 8, 2, 4, 2
EXPS = XS * CORES
ROWS, HALF, DH = 128, 64, 128
WIDTH, HEADS, KVH = 4096, 32, 2
KV = 2 * KVH * DH
PART = KV // CORES
NDOC = 8
REACH = 5
KEYS = REACH * ROWS
SHARD = 32
EPSILON = 1e-06
HIDDEN = -1e30
CHUNK = 16
LOG2E = 1.4426950408889634


def kernel(
    q_hbm, k_hbm, v_hbm, r_hbm, dl_hbm, g_hbm, w_hbm, ctx_hbm, kv_hbm,
    fbuf, tbuf, wbuf, gbuf, qv, rv, cv, lo, bias, ov, keys_t, values_one, ss, dl_ref, wv,
    send_sems, load_sems, out_sems, z_recv, f_recv, t_recv, wz_recv, wy_recv,
    wx_recv, lo_recv, g_recv, o_recv,
):
    pipe, y, zh = lax.axis_index("pipe"), lax.axis_index("y"), lax.axis_index("zh")
    x, c = lax.axis_index("x"), lax.axis_index("c")
    z = zh * SECTIONS + pipe

    def at_z(step):
        there = lax.rem(z + step, SECTIONS * ZHS)
        return {"pipe": lax.rem(there, SECTIONS), "zh": there // SECTIONS}

    def at_y(step):
        return {"y": lax.rem(y + step + YS, YS)}

    def at_x(step):
        return {"x": lax.rem(x + step, XS)}

    twin = {"c": 1 - c}
    partner = {"zh": 1 - zh}
    behind, far_behind = at_z(15), at_z(7)
    ahead, far_ahead = at_z(1), at_z(9)

    pending = []

    def when(cond, act):
        if cond is None:
            act()
        else:
            pl.when(cond)(act)

    def send(src, dst, recv, dev, cond=None):
        index = len(pending)

        def make():
            return pltpu.make_async_remote_copy(
                src_ref=src, dst_ref=dst, send_sem=send_sems.at[index],
                recv_sem=recv, device_id=dev, device_id_type=MESH,
            )

        when(cond, lambda: make().start())
        pending.append((cond, make))

    def arrive(dst, recv, cond=None):
        def act():
            pltpu.make_async_remote_copy(
                src_ref=dst, dst_ref=dst, send_sem=send_sems.at[0],
                recv_sem=recv, device_id=twin, device_id_type=MESH,
            ).wait_recv()

        when(cond, act)

    barrier = pltpu.get_barrier_semaphore()
    greeted = [partner, twin] + [at_y(k) for k in (1, -1, 3, -3)] + [at_x(k) for k in (1, 2, 3)]
    for place in (behind, far_behind, ahead, far_ahead):
        greeted += [{**place, "c": core} for core in range(CORES)]
    for dev in greeted:
        pl.semaphore_signal(barrier, inc=1, device_id=dev, device_id_type=MESH)
    spill = [(7, 6, 2), (7, 5, 3), (7, 4, 4), (6, 5, 4)]
    for a, b in ((7, 5), (5, 7)):
        @pl.when(y == a)
        def _():
            pl.semaphore_signal(barrier, inc=1, device_id={"y": b}, device_id_type=MESH)

    loads = [
        (k_hbm.at[:HALF], fbuf.at[0, zh, :, : KVH * DH]),
        (v_hbm.at[:HALF], fbuf.at[0, zh, :, KVH * DH :]),
        (k_hbm.at[HALF:], tbuf.at[0, 1 - zh, :, : KVH * DH]),
        (v_hbm.at[HALF:], tbuf.at[0, 1 - zh, :, KVH * DH :]),
        (dl_hbm, dl_ref),
        (w_hbm.at[:, :PART], wv.at[0]),
        (w_hbm.at[:, PART:], wv.at[1]),
        (q_hbm, qv),
        (r_hbm, rv),
    ]
    loads = [pltpu.make_async_copy(a, b, load_sems.at[i]) for i, (a, b) in enumerate(loads)]
    for load in loads:
        load.start()

    for d in range(1, REACH):
        @pl.when(y < d)
        def _():
            fbuf[d] = jnp.zeros(fbuf.shape[1:], fbuf.dtype)

    loads[4].wait()
    row = lax.broadcasted_iota(jnp.int32, (HALF, 1), 0)
    lane = lax.broadcasted_iota(jnp.int32, (1, KEYS), 1)
    shard = y * ZHS + zh
    for run in range(2):
        query_pos = row + (shard if run == 0 else 2 * YS * ZHS - 1 - shard) * HALF
        top = y if run == 0 else 2 * YS - 1 - y
        key_pos = top * ROWS + lax.rem(lane, ROWS) - ROWS * lax.div(lane, ROWS)
        bound, first = jnp.int32(0), jnp.zeros((HALF, 1), jnp.int32)
        for doc in range(NDOC):
            bound = bound + dl_ref[0, doc]
            first = jnp.where(query_pos >= bound, bound, first)
        seen = (key_pos >= first) & (key_pos <= query_pos)
        bias[run] = jnp.where(seen, 0.0, HIDDEN)

    extra = jnp.where((y == 7) | (y == 5), 1, 0)
    pl.semaphore_wait(barrier, len(greeted) + extra)

    for load in loads[5:7]:
        load.wait()
    for core in range(CORES):
        for place in (behind, far_behind):
            send(wv.at[core], wbuf.at[y, x, zh, c], wz_recv.at[zh, c], {**place, "c": core})
    for load in loads[:4]:
        load.wait()
    send(fbuf.at[0, zh], fbuf.at[0, zh], z_recv.at[0], partner)
    send(tbuf.at[0, 1 - zh], tbuf.at[0, 1 - zh], z_recv.at[1], partner)

    def copies(at, shift, d, half):
        slot = d + shift
        if slot < REACH:
            @pl.when(y == at)
            def _():
                pltpu.make_async_copy(fbuf.at[d, half], tbuf.at[slot, half], t_recv.at[slot, half]).start()

    def first_from_own(half):
        for k in (1, 3):
            send(fbuf.at[0, half], fbuf.at[k, half], f_recv.at[k, half], at_y(k), y + k < YS)
        for src, dst, slot in spill:
            send(fbuf.at[0, half], tbuf.at[slot, half], t_recv.at[slot, half], {"y": dst}, y == src)
        copies(7, 1, 0, half)
        copies(6, 3, 0, half)

    def second_from_own(half):
        for k in (1, 3):
            send(tbuf.at[0, half], tbuf.at[k, half], t_recv.at[k, half], at_y(-k), y >= k)

    def first_on(d, half):
        arrive(fbuf.at[d, half], f_recv.at[d, half], y >= d)
        if d % 2 == 1:
            send(fbuf.at[d, half], fbuf.at[d + 1, half], f_recv.at[d + 1, half], at_y(1), (y >= d) & (y + 1 < YS))
        copies(7, 1, d, half)
        copies(6, 3, d, half)

    def second_on(d, half):
        arrive(tbuf.at[d, half], t_recv.at[d, half], y + d < YS)
        if d % 2 == 1:
            send(tbuf.at[d, half], tbuf.at[d + 1, half], t_recv.at[d + 1, half], at_y(-1), (y + d < YS) & (y > 0))

    def w_part(r, side):
        return wbuf.at[lax.rem(y + YS - r, YS), lax.rem(x + side, XS)]

    def w_along_x(r):
        part = w_part(r, 0)
        for k in range(1, XS):
            send(part, part, wx_recv.at[r, XS - k], at_x(k))

    def w_start(h):
        for core in range(CORES):
            arrive(wbuf.at[y, x, h, core], wz_recv.at[h, core])
        part = w_part(0, 0).at[h]
        for k in (1, -1, 3, -3):
            send(part, part, wy_recv.at[k % YS, h], at_y(k))

    def w_on(r, h):
        part = w_part(r, 0).at[h]
        arrive(part, wy_recv.at[r, h])
        if r in (1, 3):
            send(part, part, wy_recv.at[r + 1, h], at_y(1))
        if r == 7:
            send(part, part, wy_recv.at[r - 1, h], at_y(-1))

    own, other = zh, 1 - zh
    first_from_own(own)
    second_from_own(other)
    send(g_hbm, gbuf, g_recv, behind)
    ss[...] = jnp.zeros_like(ss)
    near, far = ahead["zh"], 1 - ahead["zh"]
    w_start(near)
    for d in (1, 3):
        first_on(d, own)
        second_on(d, other)
    w_start(far)
    w_along_x(0)
    for r in (1, 7, 3, 5):
        w_on(r, near)
    arrive(fbuf.at[0, other], z_recv.at[0])
    first_from_own(other)
    for r in (1, 7, 3, 5):
        w_on(r, far)
        w_along_x(r)
    arrive(tbuf.at[0, own], z_recv.at[1])
    second_from_own(own)
    for d in (1, 3):
        first_on(d, other)
        second_on(d, own)
    for r in (2, 6, 4):
        w_on(r, near)
        w_on(r, far)
        w_along_x(r)
    for d in (2, 4):
        for half in range(2):
            first_on(d, half)
    for load in loads[7:]:
        load.wait()

    scale = LOG2E / math.sqrt(DH)
    last = pipe == SECTIONS - 1
    ones = jnp.ones((KEYS, DH), jnp.bfloat16)

    def add_squares(core, run, group):
        rows = pl.ds(run * HALF, HALF)
        found = ss[core, rows]
        for i in range(HEADS // KVH):
            out = lo[core, rows, pl.ds((group * (HEADS // KVH) + i) * DH, DH)].astype(jnp.float32)
            found = found + out * out
        ss[core, rows] = found

    def from_twin(run, group):
        part = lo.at[1 - c, pl.ds(run * HALF, HALF), pl.ds(group * (WIDTH // KVH), WIDTH // KVH)]
        arrive(part, lo_recv.at[run, group])
        add_squares(1 - c, run, group)

    def attend(run, group):
        buf = fbuf if run == 0 else tbuf
        own_lo = lo.at[c]
        rows = pl.ds(run * HALF, HALF)
        keys = buf[:, :, :, pl.ds(group * DH, DH)].reshape(KEYS, DH)
        values = buf[:, :, :, pl.ds((KVH + group) * DH, DH)].reshape(KEYS, DH)
        keys_t[...] = keys.T
        values_one[:, :DH] = values
        values_one[:, DH:] = ones
        per_group = HEADS // KVH

        def step(j, carry):
            base = (group * per_group + j * CHUNK) * DH
            cols = [pl.ds(pl.multiple_of(base + i * DH, DH), DH) for i in range(CHUNK)]
            queries = jnp.concatenate([qv[rows, col] for col in cols], axis=0)
            scores = jnp.dot(queries, keys_t[...], preferred_element_type=jnp.float32)
            scores = scores.reshape(CHUNK, HALF, KEYS) * scale + bias[run]
            weights = jnp.exp2(scores - jnp.max(scores, axis=2, keepdims=True))
            rounded = weights.astype(jnp.bfloat16).reshape(CHUNK * HALF, KEYS)
            mixed = jnp.dot(rounded, values_one[...], preferred_element_type=jnp.float32)
            mixed = (mixed[:, :DH] / mixed[:, DH:]).astype(jnp.bfloat16)
            for i, col in enumerate(cols):
                context = mixed[i * HALF : (i + 1) * HALF]
                cv[rows, col] = context
                out = (rv[rows, col].astype(jnp.float32) + context.astype(jnp.float32)).astype(jnp.bfloat16)
                out = jnp.where(last, jnp.zeros_like(out), out)
                own_lo[rows, col] = out
            return carry

        lax.fori_loop(0, per_group // CHUNK, step, 0)
        part = lo.at[c, rows, pl.ds(group * per_group * DH, per_group * DH)]
        send(part, part, lo_recv.at[run, group], twin)
        add_squares(c, run, group)

    outs = [
        pltpu.make_async_copy(cv.at[pl.ds(run * HALF, HALF)], ctx_hbm.at[pl.ds(run * HALF, HALF)], out_sems.at[run])
        for run in range(2)
    ]
    attend(0, 0)
    attend(0, 1)
    outs[0].start()
    for d in (2, 4):
        for half in range(2):
            second_on(d, half)
    for d in range(1, REACH):
        for half in range(2):
            arrive(tbuf.at[d, half], t_recv.at[d, half], y + d >= YS)
    attend(1, 0)
    from_twin(0, 0)
    from_twin(0, 1)
    attend(1, 1)
    outs[1].start()
    arrive(gbuf, g_recv)
    for r in range(YS):
        for side in range(1, XS):
            arrive(w_part(r, side), wx_recv.at[r, side])
    tokens, depth = CORES * HALF, WIDTH // YS
    for run in range(2):
        if run == 1:
            from_twin(1, 0)
            from_twin(1, 1)
        rows = pl.ds(run * HALF, HALF)
        squares = jnp.sum(ss[:, rows].reshape(tokens, DH), axis=1, keepdims=True)
        inverse = lax.rsqrt(squares / WIDTH + EPSILON)
        total = jnp.zeros((tokens, PART), jnp.float32)
        for i in range(YS):
            cols = pl.ds(i * depth, depth)
            part = lo[:, rows, cols].reshape(tokens, depth).astype(jnp.float32)
            weights = [wbuf[i, j, h].reshape(CORES * SHARD, PART) for h in range(ZHS) for j in range(XS)]
            weights = jnp.concatenate(weights, axis=0)
            normed = (part * inverse * gbuf[:, cols]).astype(jnp.bfloat16)
            total = total + jnp.dot(normed, weights, preferred_element_type=jnp.float32)
        ov[:, rows] = total.astype(jnp.bfloat16).reshape(CORES, HALF, PART)
        mine = kv_hbm.at[rows, pl.ds(pl.multiple_of(c * PART, PART), PART)]
        for core in range(CORES):
            send(ov.at[core, rows], mine, o_recv.at[run, c], {**ahead, "c": core})
    for out in outs:
        out.wait()
    for run in range(2):
        for core in range(CORES):
            arrive(kv_hbm.at[pl.ds(run * HALF, HALF), pl.ds(core * PART, PART)], o_recv.at[run, core])
    for cond, make in pending:
        when(cond, lambda: make().wait_send())


def on_device(queries, key_rows, value_rows, residual, doc_lengths, norm_gain, kv_weight):
    bf16, f32 = jnp.bfloat16, jnp.float32
    anywhere = pl.BlockSpec(memory_space=pl.ANY)
    dma = pltpu.SemaphoreType.DMA
    context, kv_next = pl.pallas_call(
        kernel,
        out_shape=(
            jax.ShapeDtypeStruct((ROWS, WIDTH), bf16),
            jax.ShapeDtypeStruct((ROWS, KV), bf16),
        ),
        in_specs=[anywhere] * 4 + [anywhere] + [anywhere] * 2,
        out_specs=(anywhere, anywhere),
        scratch_shapes=[
            pltpu.VMEM((REACH, ZHS, HALF, KV), bf16),
            pltpu.VMEM((REACH, ZHS, HALF, KV), bf16),
            pltpu.VMEM((YS, XS, ZHS, CORES, SHARD, PART), bf16),
            pltpu.VMEM((1, WIDTH), f32),
            pltpu.VMEM((ROWS, WIDTH), bf16),
            pltpu.VMEM((ROWS, WIDTH), bf16),
            pltpu.VMEM((ROWS, WIDTH), bf16),
            pltpu.VMEM((CORES, ROWS, WIDTH), bf16),
            pltpu.VMEM((2, HALF, KEYS), f32),
            pltpu.VMEM((CORES, ROWS, PART), bf16),
            pltpu.VMEM((DH, KEYS), bf16),
            pltpu.VMEM((KEYS, 2 * DH), bf16),
            pltpu.VMEM((CORES, ROWS, DH), f32),
            pltpu.SMEM((1, NDOC), jnp.int32),
            pltpu.VMEM((CORES, SHARD, PART), bf16),
            dma((96,)),
            dma((9,)),
            dma((2,)),
            dma((2,)),
            dma((REACH, ZHS)),
            dma((REACH, ZHS)),
            dma((ZHS, CORES)),
            dma((YS, ZHS)),
            dma((YS, XS)),
            dma((2, KVH)),
            dma(()),
            dma((2, CORES)),
        ],
        compiler_params=pltpu.CompilerParams(
            collective_id=0, has_side_effects=True, vmem_limit_bytes=60 * 2**20
        ),
    )(
        queries.reshape(ROWS, WIDTH),
        key_rows.reshape(ROWS, KVH * DH),
        value_rows.reshape(ROWS, KVH * DH),
        residual.reshape(ROWS, WIDTH),
        doc_lengths.reshape(1, NDOC),
        norm_gain,
        kv_weight.reshape(SHARD, KV),
    )
    return context.reshape(1, 1, ROWS, WIDTH), kv_next.reshape(1, 1, ROWS, KV)


def solution(mesh):
    finer = Mesh(mesh.devices.reshape(SECTIONS, YS, ZHS, XS, CORES), NAMES)
    tokens = P("pipe", ("x", "c"), ("y", "zh"), None)
    return jax.shard_map(
        on_device,
        mesh=finer,
        in_specs=(
            tokens, tokens, tokens, tokens,
            P("pipe", ("x", "c"), None),
            P("pipe", None),
            P("pipe", ("y", "zh", "x", "c"), None),
        ),
        out_specs=(tokens, tokens),
        check_vma=False,
    )
```
